256 devices in a mesh: energy: 32 (over z_lo, y, core), matrix: 8 (over x, z_hi).
Axes of the slice: x: 4, y: 4, z: 8 (z_hi: 2, z_lo: 4; z = z_hi * 4 + z_lo), core: 2. Of those that a mesh axis runs over, the one named last changes fastest.
Arguments:
- lesser: float32 [2, 2, 256, 131072], P(None, None, 'energy', 'matrix'), may hold values from -6 to 6
- greater_t: float32 [2, 2, 256, 131072], P(None, None, 'energy', 'matrix'), may hold values from -6 to 6
- panel_store: float32 [32, 256, 256], P('matrix'), may hold values from -0.1875 to 0.1875
- owner: int32 [4], replicated, may hold values from 0 to 7
- pattern: int32 [128, 4], P('matrix'), may hold values from 0 to 3, each once within a row
Outputs:
- polarization: float32 [2, 2, 256, 131072], P(None, None, 'energy', 'matrix')
- screened: float32 [2, 2, 256, 32768], P(None, None, 'energy', 'matrix')
The draws below stay inside these ranges and needn't reach their ends.
Inputs may be any that keep to these rules, and one draw needn't show every extreme that they name: Panel b is stored in slot b of device owner[b] along matrix. Each row of pattern names every block once.
All inputs are finite; a program needn't handle non-finite values.
Results may differ from the reference program's by a relative error of at most 0.000098.
Values sent between devices are 32-bit elements; how exact they have to be, the bound alone decides.
No kernel may reach another device: no remote copies, remote signals or barrier semaphores. Data moves between devices by JAX's collectives and lax.ppermute only.
A program may use at most 64 MiB of HBM per device.

```python
import math
import jax
import jax.numpy as jnp
from jax import lax

NE = 256
NB = 4
NR = 256
NC = 128
KP = 2
NEL = 131072
N_MATRIX = 8


def touch_ends(entries, rng, low, largest):
    shape = entries.shape
    place = [jax.random.randint(jax.random.fold_in(rng, axis), (), 0, shape[axis]) for axis in range(len(shape))]
    entries = entries.at[tuple(place)].set(low)
    longest = shape.index(max(shape))
    place[longest] = (place[longest] + 1) % shape[longest]
    return entries.at[tuple(place)].set(largest)


def level_of(rng, dims, cuts, low, high):
    level, own = 1.0, jax.random.fold_in(rng, 6)
    for position, blocks in cuts:
        draws = jnp.exp(jax.random.uniform(jax.random.fold_in(own, position), (blocks,), jnp.float32, low / len(cuts), high / len(cuts)))
        level = level * jnp.repeat(draws, dims[position] // blocks).reshape([-1 if axis == position else 1 for axis in range(len(dims))])
    return level


def centred(key, extent, width, bound, shards=(), kind=jnp.bfloat16):
    entries = width * jax.random.normal(key, extent, jnp.float32)
    if shards:
        entries = entries * level_of(key, extent, shards, -0.22, 0.18)
    return jnp.clip(entries, -bound, bound).astype(kind)


def setup_inputs(seed: int = 0) -> dict:
    seeds = jax.random.split(jax.random.key(seed), 6)
    lesser = centred(seeds[0], (KP, 2, NE, NEL), 1.0, 6.0, ((2, 32), (3, 8)), jnp.float32)
    greater_t = centred(seeds[1], (KP, 2, NE, NEL), 1.0, 6.0, ((2, 32), (3, 8)), jnp.float32)
    panel_store = centred(seeds[2], (NB * N_MATRIX, NR, NR), (NB * NR) ** -0.5, 0.1875, ((0, 8),), jnp.float32)
    owner = touch_ends(jax.random.randint(seeds[3], (NB,), 0, N_MATRIX), jax.random.fold_in(seeds[3], 1), 0, N_MATRIX - 1).astype(jnp.int32)
    pattern = jax.vmap(lambda own: jax.random.permutation(own, NB))(jax.random.split(seeds[4], NC)).reshape((NC, NB)).astype(jnp.int32)
    return {"lesser": lesser, "greater_t": greater_t, "panel_store": panel_store, "owner": owner, "pattern": pattern}


def correlate(left_re, left_im, right_re, right_im):
    left = lax.complex(left_re, left_im)
    right = lax.complex(right_re, right_im)
    freq_count = 2 * NE
    spectrum_left = jnp.fft.fft(left, n=freq_count, axis=1)
    spectrum_right = jnp.fft.ifft(right, n=freq_count, axis=1) * freq_count
    correl = jnp.fft.ifft(spectrum_left * spectrum_right, axis=1)[:, :NE]
    prefactor = 1.0 / math.sqrt(NE)
    return (jnp.imag(correl) * prefactor, -jnp.real(correl) * prefactor)

def reference(lesser, greater_t, panel_store, owner, pattern):
    block_size = min(4096, NEL)
    block_count = NEL // block_size

    def one_block(index):
        start = index * block_size
        left = lax.dynamic_slice_in_dim(lesser, start, block_size, 3)
        right = lax.dynamic_slice_in_dim(greater_t, start, block_size, 3)
        real_part, imag_part = correlate(left[:, 0], left[:, 1], right[:, 0], right[:, 1])
        return jnp.stack((real_part, imag_part), axis=1)
    blocks = lax.map(one_block, jnp.arange(block_count, dtype=jnp.int32))
    polarization = jnp.moveaxis(blocks, 0, 3).reshape(KP, 2, NE, NEL)
    panels = panel_store[owner * NB + jnp.arange(NB, dtype=jnp.int32)]
    shaped = polarization.reshape(KP, 2, NE, NC, NB, NR)
    chosen = jnp.take_along_axis(shaped, pattern.astype(jnp.int32)[None, None, None, :, :, None], axis=4)
    screened = jnp.einsum('brs,kyecbs->kyecr', panels, chosen, precision=lax.Precision.HIGHEST)
    return (polarization, screened.reshape(KP, 2, NE, NC * NR))
```

```python
import functools
import math

import jax
import jax.numpy as jnp
import ml_dtypes
import numpy as np
from jax import lax
from jax.experimental import pallas as pl
from jax.experimental.pallas import tpu as pltpu
from jax.sharding import Mesh, PartitionSpec as P

NB = 4
NR = 256
F32 = jnp.float32
BF16 = jnp.bfloat16


def split_table(table):
    high = table.astype(ml_dtypes.bfloat16)
    low = (table - high.astype(np.float64)).astype(ml_dtypes.bfloat16)
    return np.stack((high, low))


def make_tables(block, scale):
    length = 2 * block
    freq = np.concatenate((np.arange(0, length, 2), np.arange(1, length, 2)))
    angle = (freq[:, None] * np.arange(block)[None, :] % length) * (2.0 * math.pi / length)
    cosine, sine = np.cos(angle), np.sin(angle)
    left = np.block([[cosine, sine], [-sine, cosine]])
    right = np.block([[cosine, -sine], [sine, cosine]])
    back = np.block([[sine.T, cosine.T], [-cosine.T, sine.T]]) * (scale / length)
    return split_table(left), split_table(right), split_table(back)


def split(values):
    high = values.astype(BF16)
    return high, (values - high.astype(F32)).astype(BF16)


def dot3(table, values):
    high, low = split(values)
    dot = functools.partial(jnp.dot, preferred_element_type=F32)
    return dot(table[0], high) + (dot(table[0], low) + dot(table[1], high))


def times(a, b):
    n = a.shape[0] // 2
    ar, ai, br, bi = a[:n], a[n:], b[:n], b[n:]
    return jnp.concatenate((ar * br - ai * bi, ar * bi + ai * br))


def shifted(a):
    q = a.shape[0] // 4
    return jnp.concatenate((a[:q], -a[q : 2 * q], a[2 * q : 3 * q], -a[3 * q :]))


def pack_kernel(l_ref, g_ref, o_ref):
    for k in range(2):
        for p in range(2):
            o_ref[0, k, p] = l_ref[k, p]
            o_ref[0, k, 2 + p] = g_ref[k, p]


def correlate_kernel(left_ref, right_ref, back_ref, x_ref, o_ref):
    half = x_ref.shape[0] // 2
    width = x_ref.shape[4]

    def pair(part, first):
        re = x_ref[part * half : (part + 1) * half, 0, first]
        im = x_ref[part * half : (part + 1) * half, 0, first + 1]
        return jnp.concatenate((re.reshape(half * 8, width), im.reshape(half * 8, width)))

    l_low, l_high = dot3(left_ref, pair(0, 0)), dot3(left_ref, pair(1, 0))
    r_low, r_high = dot3(right_ref, pair(0, 2)), dot3(right_ref, pair(1, 2))
    low = times(l_low, r_low) + times(l_high, shifted(r_low) + r_high)
    high = times(l_high, r_low)
    for part, joint in enumerate((low, high)):
        out = dot3(back_ref, joint)
        o_ref[part * half : (part + 1) * half, 0, 0] = out[: half * 8].reshape(half, 8, width)
        o_ref[part * half : (part + 1) * half, 0, 1] = out[half * 8 :].reshape(half, 8, width)


def finish_kernel(pattern_ref, v_ref, x_ref, pol_ref, scr_ref, xh, xl):
    groups, rows, low_energy, piece = x_ref.shape
    columns = groups * piece // (NB * NR)
    per = piece // NR
    m = rows * low_energy
    for g in range(groups):
        pol_ref[:, :, g * piece : (g + 1) * piece] = x_ref[g]
    for c in range(columns):
        for b in range(NB):
            at = c * NB + pattern_ref[c, b]
            lane = pl.multiple_of((at % per) * NR, NR)
            high, low = split(x_ref[at // per, :, :, pl.ds(lane, NR)].reshape(m, NR))
            xh[c * m : (c + 1) * m, b * NR : (b + 1) * NR] = high
            xl[c * m : (c + 1) * m, b * NR : (b + 1) * NR] = low
    dot = functools.partial(
        lax.dot_general, dimension_numbers=(((1,), (1,)), ((), ())), preferred_element_type=F32
    )
    total = jnp.zeros((columns * m, NR), F32)
    for b in range(NB):
        cut = slice(b * NR, (b + 1) * NR)
        vh, vl = split(v_ref[b])
        total += dot(xh[:, cut], vh) + (dot(xl[:, cut], vh) + dot(xh[:, cut], vl))
    for c in range(columns):
        scr_ref[:, :, c * NR : (c + 1) * NR] = total[c * m : (c + 1) * m].reshape(rows, low_energy, NR)


def broadcast_panels(panel_store, owner):
    me = lax.axis_index("m")
    rows = NR // 8
    part = lax.axis_index(("y", "c"))
    mine = lax.dynamic_slice_in_dim(panel_store, part * rows, rows, 1)
    mine = jnp.where((owner == me)[:, None, None], mine, 0.0)
    mine = lax.psum(mine, "m")
    return lax.all_gather(mine, ("y", "c"), axis=1, tiled=True)


def local(lesser, greater_t, panel_store, owner, pattern):
    kpoints, _, local_energy, elements = lesser.shape
    axes = ("z", "y", "c")
    groups = lax.axis_size(axes)
    total_energy = groups * local_energy
    piece = elements // groups
    tables = make_tables(total_energy // 2, 1.0 / math.sqrt(total_energy))
    panels = broadcast_panels(panel_store, owner)

    packed = pl.pallas_call(
        pack_kernel,
        grid=(groups,),
        in_specs=[pl.BlockSpec((kpoints, 2, local_energy, piece), lambda j: (0, 0, 0, j))] * 2,
        out_specs=pl.BlockSpec((1, kpoints, 4, local_energy, piece), lambda j: (j, 0, 0, 0, 0)),
        out_shape=jax.ShapeDtypeStruct((groups, kpoints, 4, local_energy, piece), F32),
        name="pack",
    )(lesser, greater_t)
    pieces = lax.all_to_all(packed, axes, 0, 0, tiled=True)
    pieces, panels = lax.optimization_barrier((pieces, panels))

    width = 256
    whole = lambda t: pl.BlockSpec(t.shape, lambda k, j: (0,) * t.ndim)
    result = pl.pallas_call(
        correlate_kernel,
        grid=(kpoints, piece // width),
        in_specs=[whole(t) for t in tables]
        + [pl.BlockSpec((groups, 1, 4, local_energy, width), lambda k, j: (0, k, 0, 0, j))],
        out_specs=pl.BlockSpec((groups, 1, 2, local_energy, width), lambda k, j: (0, k, 0, 0, j)),
        out_shape=jax.ShapeDtypeStruct((groups, kpoints, 2, local_energy, piece), F32),
        compiler_params=pltpu.CompilerParams(vmem_limit_bytes=40 * 2**20),
        name="correlate",
    )(*[jnp.asarray(t) for t in tables], pieces)
    returned = lax.all_to_all(result.reshape(groups, kpoints * 2, local_energy, piece), axes, 0, 0, tiled=True)

    columns = elements // (NB * NR)
    rows = kpoints * 2
    vmem = pl.BlockSpec(memory_space=pltpu.VMEM)
    polarization, screened = pl.pallas_call(
        finish_kernel,
        in_specs=[pl.BlockSpec(memory_space=pltpu.SMEM), vmem, vmem],
        out_specs=[vmem, vmem],
        out_shape=[
            jax.ShapeDtypeStruct((rows, local_energy, elements), F32),
            jax.ShapeDtypeStruct((rows, local_energy, columns * NR), F32),
        ],
        scratch_shapes=[pltpu.VMEM((columns * rows * local_energy, NB * NR), BF16)] * 2,
        compiler_params=pltpu.CompilerParams(vmem_limit_bytes=40 * 2**20),
        name="finish",
    )(pattern, panels, returned)
    return (
        polarization.reshape(kpoints, 2, local_energy, elements),
        screened.reshape(kpoints, 2, local_energy, columns * NR),
    )


def solution(mesh):
    split_mesh = Mesh(mesh.devices.reshape(4, 4, 2, 8), ("z", "y", "c", "m"))
    energy = ("z", "y", "c")
    in_specs = (
        P(None, None, energy, "m"),
        P(None, None, energy, "m"),
        P("m", None, None),
        P(),
        P("m", None),
    )
    out_specs = (P(None, None, energy, "m"), P(None, None, energy, "m"))
    return jax.shard_map(local, mesh=split_mesh, in_specs=in_specs, out_specs=out_specs, check_vma=False)
```

```python
import functools
import math

import jax
import jax.numpy as jnp
import ml_dtypes
import numpy as np
from jax import lax
from jax.experimental import pallas as pl
from jax.experimental.pallas import tpu as pltpu
from jax.sharding import Mesh, PartitionSpec as P

NB = 4
NR = 256
F32 = jnp.float32
BF16 = jnp.bfloat16


def split_table(table):
    high = table.astype(ml_dtypes.bfloat16)
    low = (table - high.astype(np.float64)).astype(ml_dtypes.bfloat16)
    return np.stack((high, low))


def make_tables(block, scale):
    length = 2 * block
    freq = np.concatenate((np.arange(0, length, 2), np.arange(1, length, 2)))
    angle = (freq[:, None] * np.arange(block)[None, :] % length) * (2.0 * math.pi / length)
    cosine, sine = np.cos(angle), np.sin(angle)
    left = np.block([[cosine, sine], [-sine, cosine]])
    right = np.block([[cosine, -sine], [sine, cosine]])
    back = np.block([[sine.T, cosine.T], [-cosine.T, sine.T]]) * (scale / length)
    return split_table(left), split_table(right), split_table(back)


def split(values):
    high = values.astype(BF16)
    return high, (values - high.astype(F32)).astype(BF16)


def dot3(table, values):
    high, low = split(values)
    dot = functools.partial(jnp.dot, preferred_element_type=F32)
    return dot(table[0], high) + (dot(table[0], low) + dot(table[1], high))


def times(a, b):
    n = a.shape[0] // 2
    ar, ai, br, bi = a[:n], a[n:], b[:n], b[n:]
    return jnp.concatenate((ar * br - ai * bi, ar * bi + ai * br))


def shifted(a):
    q = a.shape[0] // 4
    return jnp.concatenate((a[:q], -a[q : 2 * q], a[2 * q : 3 * q], -a[3 * q :]))


def pack_kernel(l_ref, g_ref, o_ref, held, read_sems, write_sems):
    groups, _, _, _, piece = o_ref.shape
    reads = [
        pltpu.make_async_copy(
            ref.at[:, :, :, j * piece : (j + 1) * piece],
            held.at[j, :, 2 * side : 2 * side + 2],
            read_sems.at[2 * j + side],
        )
        for j in range(groups)
        for side, ref in enumerate((l_ref, g_ref))
    ]
    writes = [pltpu.make_async_copy(held.at[j], o_ref.at[j], write_sems.at[j]) for j in range(groups)]
    for copy in reads:
        copy.start()
    for j, copy in enumerate(writes):
        reads[2 * j].wait()
        reads[2 * j + 1].wait()
        copy.start()
    for copy in writes:
        copy.wait()


def correlate_kernel(left_ref, right_ref, back_ref, x_ref, o_ref):
    groups, kpoints, _, rows, piece = x_ref.shape
    half = groups // 2
    width = min(256, piece)
    for k in range(kpoints):
        for start in range(0, piece, width):
            lanes = slice(start, start + width)

            def pair(part, first):
                cut = slice(part * half, (part + 1) * half)
                re, im = x_ref[cut, k, first, :, lanes], x_ref[cut, k, first + 1, :, lanes]
                return jnp.concatenate((re.reshape(half * rows, width), im.reshape(half * rows, width)))

            l_low, l_high = dot3(left_ref, pair(0, 0)), dot3(left_ref, pair(1, 0))
            r_low, r_high = dot3(right_ref, pair(0, 2)), dot3(right_ref, pair(1, 2))
            low = times(l_low, r_low) + times(l_high, shifted(r_low) + r_high)
            high = times(l_high, r_low)
            for part, joint in enumerate((low, high)):
                out = dot3(back_ref, joint)
                cut = slice(part * half, (part + 1) * half)
                o_ref[cut, 2 * k, :, lanes] = out[: half * rows].reshape(half, rows, width)
                o_ref[cut, 2 * k + 1, :, lanes] = out[half * rows :].reshape(half, rows, width)


def finish_kernel(pattern_ref, v_ref, x_ref, pol_ref, scr_ref, xh, xl, sems):
    groups, rows, low_energy, piece = x_ref.shape
    columns = groups * piece // (NB * NR)
    per = piece // NR
    m = rows * low_energy
    copies = [
        pltpu.make_async_copy(x_ref.at[g], pol_ref.at[:, :, g * piece : (g + 1) * piece], sems.at[g])
        for g in range(groups)
    ]
    for copy in copies:
        copy.start()
    for c in range(columns):
        for b in range(NB):
            at = c * NB + pattern_ref[c, b]
            lane = pl.multiple_of((at % per) * NR, NR)
            high, low = split(x_ref[at // per, :, :, pl.ds(lane, NR)].reshape(m, NR))
            xh[c * m : (c + 1) * m, b * NR : (b + 1) * NR] = high
            xl[c * m : (c + 1) * m, b * NR : (b + 1) * NR] = low
    dot = functools.partial(
        lax.dot_general, dimension_numbers=(((1,), (1,)), ((), ())), preferred_element_type=F32
    )
    total = jnp.zeros((columns * m, NR), F32)
    for b in range(NB):
        cut = slice(b * NR, (b + 1) * NR)
        vh, vl = split(v_ref[b])
        total += dot(xh[:, cut], vh) + (dot(xl[:, cut], vh) + dot(xh[:, cut], vl))
    for c in range(columns):
        scr_ref[:, :, c * NR : (c + 1) * NR] = total[c * m : (c + 1) * m].reshape(rows, low_energy, NR)
    for copy in copies:
        copy.wait()


def partial_panels(panel_store, owner):
    me = lax.axis_index(("x", "g"))
    at = lax.axis_index("x")
    size = lax.axis_size("x")
    rows = NR // (8 * size)
    part = lax.axis_index(("y", "c"))
    mine = lax.dynamic_index_in_dim(panel_store.reshape(NB, size, 8, rows, NR), part, 2, keepdims=False)
    mine = jnp.where((owner == me)[:, None, None, None], mine, 0.0)
    total = lax.dynamic_index_in_dim(mine, at, 1, keepdims=False)
    for step in range(1, size):
        piece = lax.dynamic_index_in_dim(mine, (at + step) % size, 1, keepdims=False)
        total = total + lax.ppermute(piece, "x", [(i, (i + step) % size) for i in range(size)])
    total = total + lax.ppermute(total, "g", [(0, 1), (1, 0)])
    return lax.all_gather(total, ("y", "c"), axis=1, tiled=True)


def whole_panels(rows):
    at = lax.axis_index("x")
    size = lax.axis_size("x")
    share = rows.shape[1]
    panels = jnp.zeros((NB, NR, NR), F32)
    panels = lax.dynamic_update_slice_in_dim(panels, rows, at * share, 1)
    for step in range(1, size):
        piece = lax.ppermute(rows, "x", [(i, (i + step) % size) for i in range(size)])
        panels = lax.dynamic_update_slice_in_dim(panels, piece, (at - step) % size * share, 1)
    return panels


def local(lesser, greater_t, panel_store, owner, pattern):
    kpoints, _, local_energy, elements = lesser.shape
    axes = ("z", "y", "c")
    groups = lax.axis_size(axes)
    total_energy = groups * local_energy
    piece = elements // groups
    tables = make_tables(total_energy // 2, 1.0 / math.sqrt(total_energy))
    panel_rows = partial_panels(panel_store, owner)
    vmem = pl.BlockSpec(memory_space=pltpu.VMEM)
    hbm = pl.BlockSpec(memory_space=pltpu.HBM)
    params = pltpu.CompilerParams(vmem_limit_bytes=24 * 2**20)

    packed = pl.pallas_call(
        pack_kernel,
        in_specs=[hbm, hbm],
        out_specs=hbm,
        out_shape=jax.ShapeDtypeStruct((groups, kpoints, 4, local_energy, piece), F32),
        scratch_shapes=[
            pltpu.VMEM((groups, kpoints, 4, local_energy, piece), F32),
            pltpu.SemaphoreType.DMA((2 * groups,)),
            pltpu.SemaphoreType.DMA((groups,)),
        ],
        compiler_params=pltpu.CompilerParams(vmem_limit_bytes=60 * 2**20),
        name="pack",
    )(lesser, greater_t)
    pieces = lax.all_to_all(packed, axes, 0, 0, tiled=True)
    pieces, panel_rows = lax.optimization_barrier((pieces, panel_rows))
    panels = whole_panels(panel_rows)

    rows = kpoints * 2
    result = pl.pallas_call(
        correlate_kernel,
        in_specs=[vmem] * 4,
        out_specs=vmem,
        out_shape=jax.ShapeDtypeStruct((groups, rows, local_energy, piece), F32),
        compiler_params=params,
        name="correlate",
    )(*[jnp.asarray(t) for t in tables], pieces)
    returned = lax.all_to_all(result, axes, 0, 0, tiled=True)

    columns = elements // (NB * NR)
    polarization, screened = pl.pallas_call(
        finish_kernel,
        in_specs=[pl.BlockSpec(memory_space=pltpu.SMEM), vmem, vmem],
        out_specs=[hbm, vmem],
        out_shape=[
            jax.ShapeDtypeStruct((rows, local_energy, elements), F32),
            jax.ShapeDtypeStruct((rows, local_energy, columns * NR), F32),
        ],
        scratch_shapes=[pltpu.VMEM((columns * rows * local_energy, NB * NR), BF16)] * 2
        + [pltpu.SemaphoreType.DMA((groups,))],
        compiler_params=params,
        name="finish",
    )(pattern, panels, returned)
    return (
        polarization.reshape(kpoints, 2, local_energy, elements),
        screened.reshape(kpoints, 2, local_energy, columns * NR),
    )


def solution(mesh):
    split_mesh = Mesh(mesh.devices.reshape(4, 4, 2, 4, 2), ("z", "y", "c", "x", "g"))
    energy, matrix = ("z", "y", "c"), ("x", "g")
    in_specs = (
        P(None, None, energy, matrix),
        P(None, None, energy, matrix),
        P(matrix, None, None),
        P(),
        P(matrix, None),
    )
    out_specs = (P(None, None, energy, matrix), P(None, None, energy, matrix))
    return jax.shard_map(local, mesh=split_mesh, in_specs=in_specs, out_specs=out_specs, check_vma=False)
```

```python
import functools
import math

import jax
import jax.numpy as jnp
import ml_dtypes
import numpy as np
from jax import lax
from jax.experimental import pallas as pl
from jax.experimental.pallas import tpu as pltpu
from jax.sharding import Mesh, PartitionSpec as P

NB = 4
NR = 256
BLOCKS = 4
F32 = jnp.float32
BF16 = jnp.bfloat16


def split_table(table):
    high = table.astype(ml_dtypes.bfloat16)
    low = (table - high.astype(np.float64)).astype(ml_dtypes.bfloat16)
    return np.concatenate((high, high, low), axis=1)


def make_tables(block, scale):
    length = 2 * block
    freq = np.concatenate((np.arange(0, length, 2), np.arange(1, length, 2)))
    angle = (freq[:, None] * np.arange(block)[None, :] % length) * (2.0 * math.pi / length)
    cosine, sine = np.cos(angle), np.sin(angle)
    left = np.block([[cosine, sine], [-sine, cosine]])
    right = np.block([[cosine, -sine], [sine, cosine]])
    back = np.block([[sine.T, cosine.T], [-cosine.T, sine.T]]) * (scale / length)
    return split_table(left), split_table(right), split_table(back)


def split(values):
    high = values.astype(BF16)
    return high, (values - high.astype(F32)).astype(BF16)


def dot3(table, values):
    high, low = split(values)
    return jnp.dot(table[...], jnp.concatenate((high, low, high)), preferred_element_type=F32)


def times(a, b):
    n = a.shape[0] // 2
    ar, ai, br, bi = a[:n], a[n:], b[:n], b[n:]
    return jnp.concatenate((ar * br - ai * bi, ar * bi + ai * br))


def shifted(a):
    q = a.shape[0] // 4
    return jnp.concatenate((a[:q], -a[q : 2 * q], a[2 * q : 3 * q], -a[3 * q :]))


def pack_kernel(l_ref, g_ref, o_ref, held, read_sems, write_sems):
    groups, _, _, _, piece = o_ref.shape
    parts, _, _, _, span = held.shape
    reads = [
        pltpu.make_async_copy(
            ref.at[:, :, :, i * span : (i + 1) * span],
            held.at[i, :, 2 * side : 2 * side + 2],
            read_sems.at[2 * i + side],
        )
        for i in range(parts)
        for side, ref in enumerate((l_ref, g_ref))
    ]
    for copy in reads:
        copy.start()
    writes = []
    for i in range(parts):
        reads[2 * i].wait()
        reads[2 * i + 1].wait()
        for j in range(span // piece):
            at = i * (span // piece) + j
            source = held.at[i, :, :, :, j * piece : (j + 1) * piece]
            writes.append(pltpu.make_async_copy(source, o_ref.at[at], write_sems.at[at]))
            writes[-1].start()
    for copy in writes:
        copy.wait()


def correlate_kernel(*refs):
    stored, (x_ref, out_ref), held = refs[:3], refs[3:5], refs[5:8]
    left_ref, right_ref, back_ref = held
    x, o, read_sems, write_sems = refs[8:]
    tiles, groups, _, rows, width = x.shape
    share = groups // BLOCKS
    size = share * rows
    per = tiles // x_ref.shape[1]
    reads, writes = [], []
    for t in range(tiles):
        k, lanes = t // per, slice(t % per * width, (t % per + 1) * width)
        reads.append(pltpu.make_async_copy(x_ref.at[:, k, :, :, lanes], x.at[t], read_sems.at[t]))
        writes.append(pltpu.make_async_copy(o.at[t], out_ref.at[:, 2 * k : 2 * k + 2, :, lanes], write_sems.at[t]))
    fetches = [pltpu.make_async_copy(stored[i], held[i], read_sems.at[tiles + i]) for i in range(3)]
    for copy in (reads[0], *fetches, *reads[1:]):
        copy.start()
    for copy in fetches:
        copy.wait()
    for t in range(tiles):
        reads[t].wait()

        def pair(part, first):
            cut = slice(part * share, (part + 1) * share)
            re, im = x[t, cut, first], x[t, cut, first + 1]
            return jnp.concatenate((re.reshape(size, width), im.reshape(size, width)))

        lefts = [dot3(left_ref, pair(i, 0)) for i in range(BLOCKS)]
        rights = [dot3(right_ref, pair(i, 2)) for i in range(BLOCKS)]
        windows = rights[:1] + [shifted(rights[i - 1]) + rights[i] for i in range(1, BLOCKS)]
        for part in range(BLOCKS):
            joint = times(lefts[part], windows[0])
            for i in range(part + 1, BLOCKS):
                joint = joint + times(lefts[i], windows[i - part])
            out = dot3(back_ref, joint)
            cut = slice(part * share, (part + 1) * share)
            o[t, cut, 0] = out[:size].reshape(share, rows, width)
            o[t, cut, 1] = out[size:].reshape(share, rows, width)
        writes[t].start()
    for copy in writes:
        copy.wait()


def finish_kernel(pattern_ref, stored_ref, x_ref, pol_ref, scr_ref, xh, xl, v_ref, sems):
    groups, rows, low_energy, piece = x_ref.shape
    columns = groups * piece // (NB * NR)
    per = piece // NR
    m = rows * low_energy
    copies = [
        pltpu.make_async_copy(x_ref.at[g], pol_ref.at[:, :, g * piece : (g + 1) * piece], sems.at[g])
        for g in range(groups)
    ]
    fetch = pltpu.make_async_copy(stored_ref, v_ref, sems.at[groups])
    fetch.start()
    for copy in copies:
        copy.start()
    for c in range(columns):
        for b in range(NB):
            at = c * NB + pattern_ref[c, b]
            lane = pl.multiple_of((at % per) * NR, NR)
            high, low = split(x_ref[at // per, :, :, pl.ds(lane, NR)].reshape(m, NR))
            xh[c * m : (c + 1) * m, b * NR : (b + 1) * NR] = high
            xl[c * m : (c + 1) * m, b * NR : (b + 1) * NR] = low
    dot = functools.partial(
        lax.dot_general, dimension_numbers=(((1,), (1,)), ((), ())), preferred_element_type=F32
    )
    fetch.wait()
    total = dot(xh[...], v_ref[0]) + (dot(xl[...], v_ref[0]) + dot(xh[...], v_ref[1]))
    for c in range(columns):
        scr_ref[:, :, c * NR : (c + 1) * NR] = total[c * m : (c + 1) * m].reshape(rows, low_energy, NR)
    for copy in copies:
        copy.wait()


def partial_panels(panel_store, owner):
    me = lax.axis_index(("x", "g"))
    at = lax.axis_index("x")
    size = lax.axis_size("x")
    rows = NR // (8 * size)
    part = lax.axis_index(("y", "c"))
    mine = lax.dynamic_index_in_dim(panel_store.reshape(NB, size, 8, rows, NR), part, 2, keepdims=False)
    mine = jnp.where((owner == me)[:, None, None, None], mine, 0.0)
    total = lax.dynamic_index_in_dim(mine, at, 1, keepdims=False)
    for step in range(1, size):
        piece = lax.dynamic_index_in_dim(mine, (at + step) % size, 1, keepdims=False)
        total = total + lax.ppermute(piece, "x", [(i, (i + step) % size) for i in range(size)])
    total = total + lax.ppermute(total, "g", [(0, 1), (1, 0)])
    return lax.all_gather(total, ("y", "c"), axis=1, tiled=True)


def panels_kernel(place_ref, *refs):
    *pieces, v_ref = refs
    count = len(pieces)
    share = pieces[0].shape[1]
    for step, piece in enumerate(pieces):
        row = pl.multiple_of((place_ref[0] + count - step) % count * share, share)
        for b in range(NB):
            high, low = split(piece[b])
            v_ref[0, pl.ds(row, share), b * NR : (b + 1) * NR] = high
            v_ref[1, pl.ds(row, share), b * NR : (b + 1) * NR] = low


def whole_panels(rows):
    size = lax.axis_size("x")
    pieces = [rows]
    for step in range(1, size):
        pieces.append(lax.ppermute(rows, "x", [(i, (i + step) % size) for i in range(size)]))
    vmem = pl.BlockSpec(memory_space=pltpu.VMEM)
    return pl.pallas_call(
        panels_kernel,
        in_specs=[pl.BlockSpec(memory_space=pltpu.SMEM)] + [vmem] * size,
        out_specs=vmem,
        out_shape=jax.ShapeDtypeStruct((2, NR, NB * NR), BF16),
        compiler_params=pltpu.CompilerParams(vmem_limit_bytes=56 * 2**20),
        name="panels",
    )(lax.axis_index("x").astype(jnp.int32).reshape(1), *pieces)


def local(lesser, greater_t, panel_store, owner, pattern):
    kpoints, _, local_energy, elements = lesser.shape
    axes = ("z", "y", "c")
    groups = lax.axis_size(axes)
    total_energy = groups * local_energy
    piece = elements // groups
    tables = make_tables(total_energy // BLOCKS, 1.0 / math.sqrt(total_energy))
    panel_rows = partial_panels(panel_store, owner)
    vmem = pl.BlockSpec(memory_space=pltpu.VMEM)
    hbm = pl.BlockSpec(memory_space=pltpu.HBM)
    params = pltpu.CompilerParams(vmem_limit_bytes=24 * 2**20)

    parts = 4
    packed = pl.pallas_call(
        pack_kernel,
        in_specs=[hbm, hbm],
        out_specs=hbm,
        out_shape=jax.ShapeDtypeStruct((groups, kpoints, 4, local_energy, piece), F32),
        scratch_shapes=[
            pltpu.VMEM((parts, kpoints, 4, local_energy, elements // parts), F32),
            pltpu.SemaphoreType.DMA((2 * parts,)),
            pltpu.SemaphoreType.DMA((groups,)),
        ],
        compiler_params=pltpu.CompilerParams(vmem_limit_bytes=60 * 2**20),
        name="pack",
    )(lesser, greater_t)
    pieces = lax.all_to_all(packed, axes, 0, 0, tiled=True)
    pieces, panel_rows = lax.optimization_barrier((pieces, panel_rows))
    panels = whole_panels(panel_rows)

    rows = kpoints * 2
    width = 256
    tiles = kpoints * (piece // width)
    result = pl.pallas_call(
        correlate_kernel,
        in_specs=[hbm] * 4,
        out_specs=hbm,
        out_shape=jax.ShapeDtypeStruct((groups, rows, local_energy, piece), F32),
        scratch_shapes=[pltpu.VMEM(t.shape, BF16) for t in tables]
        + [
            pltpu.VMEM((tiles, groups, 4, local_energy, width), F32),
            pltpu.VMEM((tiles, groups, 2, local_energy, width), F32),
            pltpu.SemaphoreType.DMA((tiles + 3,)),
            pltpu.SemaphoreType.DMA((tiles,)),
        ],
        compiler_params=pltpu.CompilerParams(vmem_limit_bytes=56 * 2**20),
        name="correlate",
    )(*[jnp.asarray(t) for t in tables], pieces)
    returned = lax.all_to_all(result, axes, 0, 0, tiled=True)

    columns = elements // (NB * NR)
    polarization, screened = pl.pallas_call(
        finish_kernel,
        in_specs=[pl.BlockSpec(memory_space=pltpu.SMEM), hbm, vmem],
        out_specs=[hbm, vmem],
        out_shape=[
            jax.ShapeDtypeStruct((rows, local_energy, elements), F32),
            jax.ShapeDtypeStruct((rows, local_energy, columns * NR), F32),
        ],
        scratch_shapes=[pltpu.VMEM((columns * rows * local_energy, NB * NR), BF16)] * 2
        + [pltpu.VMEM((2, NR, NB * NR), BF16), pltpu.SemaphoreType.DMA((groups + 1,))],
        compiler_params=params,
        name="finish",
    )(pattern, panels, returned)
    return (
        polarization.reshape(kpoints, 2, local_energy, elements),
        screened.reshape(kpoints, 2, local_energy, columns * NR),
    )


def solution(mesh):
    split_mesh = Mesh(mesh.devices.reshape(4, 4, 2, 4, 2), ("z", "y", "c", "x", "g"))
    energy, matrix = ("z", "y", "c"), ("x", "g")
    in_specs = (
        P(None, None, energy, matrix),
        P(None, None, energy, matrix),
        P(matrix, None, None),
        P(),
        P(matrix, None),
    )
    out_specs = (P(None, None, energy, matrix), P(None, None, energy, matrix))
    return jax.shard_map(local, mesh=split_mesh, in_specs=in_specs, out_specs=out_specs, check_vma=False)
```

```python
import functools
import math

import jax
import jax.numpy as jnp
import ml_dtypes
import numpy as np
from jax import lax
from jax.experimental import pallas as pl
from jax.experimental.pallas import tpu as pltpu
from jax.sharding import Mesh, PartitionSpec as P

NB = 4
NR = 256
BLOCKS = 4
F32 = jnp.float32
BF16 = jnp.bfloat16


def split_table(table):
    high = table.astype(ml_dtypes.bfloat16)
    low = (table - high.astype(np.float64)).astype(ml_dtypes.bfloat16)
    return np.concatenate((high, high, low), axis=1)


def make_tables(block, scale):
    length = 2 * block
    freq = np.concatenate((np.arange(0, length, 2), np.arange(1, length, 2)))
    angle = (freq[:, None] * np.arange(block)[None, :] % length) * (2.0 * math.pi / length)
    cosine, sine = np.cos(angle), np.sin(angle)
    left = np.block([[cosine, sine], [-sine, cosine]])
    right = np.block([[cosine, -sine], [sine, cosine]])
    back = np.block([[sine.T, cosine.T], [-cosine.T, sine.T]]) * (scale / length)
    return split_table(left), split_table(right), split_table(back)


def split(values):
    high = values.astype(BF16)
    return high, (values - high.astype(F32)).astype(BF16)


def dot3(table, values):
    high, low = split(values)
    return jnp.dot(table[...], jnp.concatenate((high, low, high)), preferred_element_type=F32)


def times(a, b):
    n = a.shape[0] // 2
    ar, ai, br, bi = a[:n], a[n:], b[:n], b[n:]
    return jnp.concatenate((ar * br - ai * bi, ar * bi + ai * br))


def shifted(a):
    q = a.shape[0] // 4
    return jnp.concatenate((a[:q], -a[q : 2 * q], a[2 * q : 3 * q], -a[3 * q :]))


def pack_kernel(l_ref, g_ref, o_ref, held, read_sems, write_sems):
    groups, _, _, _, piece = o_ref.shape
    parts, _, _, _, span = held.shape
    reads = [
        pltpu.make_async_copy(
            ref.at[:, :, :, i * span : (i + 1) * span],
            held.at[i, :, 2 * side : 2 * side + 2],
            read_sems.at[2 * i + side],
        )
        for i in range(parts)
        for side, ref in enumerate((l_ref, g_ref))
    ]
    for copy in reads:
        copy.start()
    writes = []
    for i in range(parts):
        reads[2 * i].wait()
        reads[2 * i + 1].wait()
        for j in range(span // piece):
            at = i * (span // piece) + j
            source = held.at[i, :, :, :, j * piece : (j + 1) * piece]
            writes.append(pltpu.make_async_copy(source, o_ref.at[at], write_sems.at[at]))
            writes[-1].start()
    for copy in writes:
        copy.wait()


def correlate_kernel(*refs):
    stored, (x_ref, out_ref), held = refs[:3], refs[3:5], refs[5:8]
    left_ref, right_ref, back_ref = held
    x, o, read_sems, write_sems = refs[8:]
    tiles, share, _, _, rows, width = x.shape
    size = share * rows
    per = tiles // x_ref.shape[2]
    reads, writes = [], []
    for t in range(tiles):
        k, lanes = t // per, slice(t % per * width, (t % per + 1) * width)
        reads.append(pltpu.make_async_copy(x_ref.at[:, :, k, :, :, lanes], x.at[t], read_sems.at[t]))
        writes.append(pltpu.make_async_copy(o.at[t], out_ref.at[:, :, 2 * k : 2 * k + 2, :, lanes], write_sems.at[t]))
    fetches = [pltpu.make_async_copy(stored[i], held[i], read_sems.at[tiles + i]) for i in range(3)]
    for copy in (reads[0], *fetches, *reads[1:]):
        copy.start()
    for copy in fetches:
        copy.wait()
    for t in range(tiles):
        reads[t].wait()

        def pair(part, first):
            re, im = x[t, :, part, first], x[t, :, part, first + 1]
            return jnp.concatenate((re.reshape(size, width), im.reshape(size, width)))

        lefts = [dot3(left_ref, pair(i, 0)) for i in range(BLOCKS)]
        rights = [dot3(right_ref, pair(i, 2)) for i in range(BLOCKS)]
        windows = rights[:1] + [shifted(rights[i - 1]) + rights[i] for i in range(1, BLOCKS)]
        for part in range(BLOCKS):
            joint = times(lefts[part], windows[0])
            for i in range(part + 1, BLOCKS):
                joint = joint + times(lefts[i], windows[i - part])
            out = dot3(back_ref, joint)
            o[t, :, part, 0] = out[:size].reshape(share, rows, width)
            o[t, :, part, 1] = out[size:].reshape(share, rows, width)
        writes[t].start()
    for copy in writes:
        copy.wait()


def finish_kernel(pattern_ref, stored_ref, x_ref, pol_ref, scr_ref, xh, xl, v_ref, sems):
    groups, rows, low_energy, piece = x_ref.shape
    columns = groups * piece // (NB * NR)
    per = piece // NR
    m = rows * low_energy
    copies = [
        pltpu.make_async_copy(x_ref.at[g], pol_ref.at[:, :, g * piece : (g + 1) * piece], sems.at[g])
        for g in range(groups)
    ]
    fetch = pltpu.make_async_copy(stored_ref, v_ref, sems.at[groups])
    fetch.start()
    for copy in copies:
        copy.start()
    dot = functools.partial(
        lax.dot_general, dimension_numbers=(((1,), (1,)), ((), ())), preferred_element_type=F32
    )

    def gather(first, last):
        for c in range(first, last):
            for b in range(NB):
                at = c * NB + pattern_ref[c, b]
                lane = pl.multiple_of((at % per) * NR, NR)
                high, low = split(x_ref[at // per, :, :, pl.ds(lane, NR)].reshape(m, NR))
                xh[c * m : (c + 1) * m, b * NR : (b + 1) * NR] = high
                xl[c * m : (c + 1) * m, b * NR : (b + 1) * NR] = low

    def product(first, last):
        cut = slice(first * m, last * m)
        total = dot(xh[cut], v_ref[0]) + (dot(xl[cut], v_ref[0]) + dot(xh[cut], v_ref[1]))
        for c in range(first, last):
            row = (c - first) * m
            scr_ref[:, :, c * NR : (c + 1) * NR] = total[row : row + m].reshape(rows, low_energy, NR)

    group = columns // 2
    gather(0, group)
    fetch.wait()
    for first in range(0, columns, group):
        if first + group < columns:
            gather(first + group, first + 2 * group)
        product(first, first + group)
    for copy in copies:
        copy.wait()


def partial_panels(panel_store, owner):
    me = lax.axis_index(("x", "g"))
    at = lax.axis_index("x")
    size = lax.axis_size("x")
    rows = NR // (8 * size)
    part = lax.axis_index(("y", "c"))
    mine = lax.dynamic_index_in_dim(panel_store.reshape(NB, size, 8, rows, NR), part, 2, keepdims=False)
    mine = jnp.where((owner == me)[:, None, None, None], mine, 0.0)
    total = lax.dynamic_index_in_dim(mine, at, 1, keepdims=False)
    for step in range(1, size):
        piece = lax.dynamic_index_in_dim(mine, (at + step) % size, 1, keepdims=False)
        total = total + lax.ppermute(piece, "x", [(i, (i + step) % size) for i in range(size)])
    total = total + lax.ppermute(total, "g", [(0, 1), (1, 0)])
    return lax.all_gather(total, ("y", "c"), axis=1, tiled=True)


def panels_kernel(place_ref, *refs):
    *pieces, v_ref = refs
    count = len(pieces)
    share = pieces[0].shape[1]
    for step, piece in enumerate(pieces):
        row = pl.multiple_of((place_ref[0] + count - step) % count * share, share)
        for b in range(NB):
            high, low = split(piece[b])
            v_ref[0, pl.ds(row, share), b * NR : (b + 1) * NR] = high
            v_ref[1, pl.ds(row, share), b * NR : (b + 1) * NR] = low


def whole_panels(rows):
    size = lax.axis_size("x")
    pieces = [rows]
    for step in range(1, size):
        pieces.append(lax.ppermute(rows, "x", [(i, (i + step) % size) for i in range(size)]))
    vmem = pl.BlockSpec(memory_space=pltpu.VMEM)
    return pl.pallas_call(
        panels_kernel,
        in_specs=[pl.BlockSpec(memory_space=pltpu.SMEM)] + [vmem] * size,
        out_specs=vmem,
        out_shape=jax.ShapeDtypeStruct((2, NR, NB * NR), BF16),
        compiler_params=pltpu.CompilerParams(vmem_limit_bytes=56 * 2**20),
        name="panels",
    )(lax.axis_index("x").astype(jnp.int32).reshape(1), *pieces)


def local(lesser, greater_t, panel_store, owner, pattern):
    kpoints, _, local_energy, elements = lesser.shape
    axes = ("y", "c", "z")
    groups = lax.axis_size(axes)
    total_energy = groups * local_energy
    piece = elements // groups
    tables = make_tables(total_energy // BLOCKS, 1.0 / math.sqrt(total_energy))
    panel_rows = partial_panels(panel_store, owner)
    vmem = pl.BlockSpec(memory_space=pltpu.VMEM)
    hbm = pl.BlockSpec(memory_space=pltpu.HBM)
    params = pltpu.CompilerParams(vmem_limit_bytes=24 * 2**20)

    parts = 4
    packed = pl.pallas_call(
        pack_kernel,
        in_specs=[hbm, hbm],
        out_specs=hbm,
        out_shape=jax.ShapeDtypeStruct((groups, kpoints, 4, local_energy, piece), F32),
        scratch_shapes=[
            pltpu.VMEM((parts, kpoints, 4, local_energy, elements // parts), F32),
            pltpu.SemaphoreType.DMA((2 * parts,)),
            pltpu.SemaphoreType.DMA((groups,)),
        ],
        compiler_params=pltpu.CompilerParams(vmem_limit_bytes=60 * 2**20),
        name="pack",
    )(lesser, greater_t)
    pieces = lax.all_to_all(packed, axes, 0, 0, tiled=True)
    pieces, panel_rows = lax.optimization_barrier((pieces, panel_rows))
    panels = whole_panels(panel_rows)

    rows = kpoints * 2
    width = 256
    tiles = kpoints * (piece // width)
    result = pl.pallas_call(
        correlate_kernel,
        in_specs=[hbm] * 4,
        out_specs=hbm,
        out_shape=jax.ShapeDtypeStruct((groups // BLOCKS, BLOCKS, rows, local_energy, piece), F32),
        scratch_shapes=[pltpu.VMEM(t.shape, BF16) for t in tables]
        + [
            pltpu.VMEM((tiles, groups // BLOCKS, BLOCKS, 4, local_energy, width), F32),
            pltpu.VMEM((tiles, groups // BLOCKS, BLOCKS, 2, local_energy, width), F32),
            pltpu.SemaphoreType.DMA((tiles + 3,)),
            pltpu.SemaphoreType.DMA((tiles,)),
        ],
        compiler_params=pltpu.CompilerParams(vmem_limit_bytes=56 * 2**20),
        name="correlate",
    )(*[jnp.asarray(t) for t in tables], pieces.reshape(groups // BLOCKS, BLOCKS, kpoints, 4, local_energy, piece))
    returned = lax.all_to_all(result.reshape(groups, rows, local_energy, piece), axes, 0, 0, tiled=True)

    columns = elements // (NB * NR)
    polarization, screened = pl.pallas_call(
        finish_kernel,
        in_specs=[pl.BlockSpec(memory_space=pltpu.SMEM), hbm, vmem],
        out_specs=[hbm, vmem],
        out_shape=[
            jax.ShapeDtypeStruct((rows, local_energy, elements), F32),
            jax.ShapeDtypeStruct((rows, local_energy, columns * NR), F32),
        ],
        scratch_shapes=[pltpu.VMEM((columns * rows * local_energy, NB * NR), BF16)] * 2
        + [pltpu.VMEM((2, NR, NB * NR), BF16), pltpu.SemaphoreType.DMA((groups + 1,))],
        compiler_params=params,
        name="finish",
    )(pattern, panels, returned)
    return (
        polarization.reshape(kpoints, 2, local_energy, elements),
        screened.reshape(kpoints, 2, local_energy, columns * NR),
    )


def solution(mesh):
    split_mesh = Mesh(mesh.devices.reshape(4, 4, 2, 4, 2), ("z", "y", "c", "x", "g"))
    energy, matrix = ("z", "y", "c"), ("x", "g")
    in_specs = (
        P(None, None, energy, matrix),
        P(None, None, energy, matrix),
        P(matrix, None, None),
        P(),
        P(matrix, None),
    )
    out_specs = (P(None, None, energy, matrix), P(None, None, energy, matrix))
    return jax.shard_map(local, mesh=split_mesh, in_specs=in_specs, out_specs=out_specs, check_vma=False)
```
